32 devices in a mesh: member: 4 (over y, x), space: 8 (over z, core).
Axes of the slice: x: 2, y: 2, z: 4, core: 2. Of those that a mesh axis runs over, the one named last changes fastest.
Arguments:
- grid_in: bfloat16 [4, 8192, 256], P('member', 'space'), may hold values from -6 to 6
- mesh_embed: bfloat16 [2048, 512], P('space'), may hold values from -6 to 6
- g2m_src: int32 [8, 8, 256], P('space'), may hold values from 0 to 1023
- g2m_dst: int32 [8, 8, 256], P('space'), may hold values from 0 to 255
- g2m_own_src: int32 [8, 1536], P('space'), may hold values from 0 to 1023
- g2m_own_dst: int32 [8, 1536], P('space'), may hold values from 0 to 255
- g2m_len: int32 [8, 8], P(None, 'space'), may hold values from 0 to 1536, as said below
- mesh_nbr: int32 [2048, 32], P('space'), may hold values from 0 to 383
- halo_rows: int32 [8, 16], P('space'), may hold values from 0 to 255
- m2g_src: int32 [8, 8, 256], P('space'), may hold values from 0 to 255
- m2g_dst: int32 [8, 8, 256], P('space'), may hold values from 0 to 1023
- m2g_own_src: int32 [8, 2560], P('space'), may hold values from 0 to 255
- m2g_own_dst: int32 [8, 2560], P('space'), may hold values from 0 to 1023
- m2g_len: int32 [8, 8], P(None, 'space'), may hold values from 0 to 2560, as said below
- w_embed: bfloat16 [256, 512], replicated, may hold values from -0.375 to 0.375
- w_send: bfloat16 [512, 512], replicated, may hold values from -0.25 to 0.25
- w_mesh: bfloat16 [512, 512], replicated, may hold values from -0.25 to 0.25
- attn_gain: float32 [512], replicated, may hold values from 0.1 to 1.9
- w_query: bfloat16 [512, 512], P('member')
- w_key: bfloat16 [512, 512], P('member')
- w_value: bfloat16 [512, 512], P('member'), may hold values from -0.25 to 0.25
- w_project: bfloat16 [512, 512], P('member'), may hold values from -0.25 to 0.25
- mlp_gain: float32 [512], replicated, may hold values from 0.1 to 1.9
- w_up: bfloat16 [512, 2048], P('member'), may hold values from -0.25 to 0.25
- w_down: bfloat16 [2048, 512], P('member'), may hold values from -0.125 to 0.125
- w_return: bfloat16 [512, 512], replicated, may hold values from -0.25 to 0.25
- w_grid: bfloat16 [512, 512], replicated, may hold values from -0.25 to 0.25
- w_skip: bfloat16 [512, 512], replicated, may hold values from -0.25 to 0.25
- w_out: bfloat16 [512, 84], replicated, may hold values from -0.25 to 0.25
Outputs:
- denoised: bfloat16 [4, 84, 8192], P('member', None, 'space')
The draws below stay inside these ranges and needn't reach their ends.
Inputs may be any that keep to these rules, and one draw needn't show every extreme that they name: Pairs with |s - d| > 1 are empty (length 0). For |s - d| = 1 slot j carries an edge exactly when j < g2m_len[s, d] <= 256; on the diagonal, slot j of g2m_own_src and g2m_own_dst carries an edge exactly when j < g2m_len[p, p] <= 1536. Other slots hold arbitrary indices. The bands at the two ends of the axis (1 at each) receive the most edges. Pairs with |s - d| > 1 are empty (length 0). For |s - d| = 1 slot j carries an edge exactly when j < m2g_len[s, d] <= 256; on the diagonal, slot j of m2g_own_src and m2g_own_dst carries an edge exactly when j < m2g_len[p, p] <= 2560. Other slots hold arbitrary indices. The bands at the two ends of the axis (1 at each) receive the most edges.
All inputs are finite; a program needn't handle non-finite values.
Results may differ from the reference program's by a relative error of at most 0.015.
Values may be sent and summed in bfloat16 or wider, within the bound.
A program may use at most 64 MiB of HBM per device.

```python
import math
import jax
import jax.numpy as jnp
from jax import lax

D = 512
F_IN = 256
F_OUT = 84
H = 4
DH = 128
FFN = 2048
K_NBR = 32
G_DEV = 1024
M_DEV = 256
SLOTS = 256
G2M_OWN = 1536
M2G_OWN = 2560
HB = 16
BANDS = 8
MEMBERS = 4
GRID = 8192
MESH = 2048


def pair_lengths(key, own_capacity):
    sender = lax.broadcasted_iota(jnp.int32, (BANDS, BANDS), 0)
    target = lax.broadcasted_iota(jnp.int32, (BANDS, BANDS), 1)
    heavy = (target < BANDS // 8) | (target >= BANDS - BANDS // 8)
    spread = jax.random.randint(key, (BANDS, BANDS), 0, 1 << 20)
    diagonal = jnp.where(heavy, own_capacity, own_capacity // 2 + spread % (own_capacity // 4 + 1))
    nearby = jnp.where(heavy, SLOTS, SLOTS // 4 + spread % (SLOTS // 4 + 1))
    apart = jnp.abs(sender - target)
    return jnp.where(apart == 0, diagonal, jnp.where(apart == 1, nearby, 0)).astype(jnp.int32)


def draw_g2m_len(key, part):
    return pair_lengths(jax.random.fold_in(key, 11), G2M_OWN)


def draw_m2g_len(key, part):
    return pair_lengths(jax.random.fold_in(key, 12), M2G_OWN)


def draw_mesh_nbr(key, part):
    first = jax.random.fold_in(key, 21)
    second = jax.random.fold_in(key, 22)
    third = jax.random.fold_in(key, 23)
    shape = (MESH, K_NBR)
    picker = jax.random.randint(first, shape, 0, 4)
    local_pick = jax.random.randint(second, shape, 0, M_DEV)
    remote_pick = M_DEV + jax.random.randint(third, shape, 0, BANDS * HB)
    return jnp.where(picker == 0, remote_pick, local_pick).astype(jnp.int32)


def head_weight(key, which):
    own_part = jax.random.normal(jax.random.fold_in(key, 32 + which), (D, D), jnp.float32)
    mixed = own_part / jnp.sqrt(jnp.float32(D))
    return mixed.astype(jnp.bfloat16)


def draw_w_query(key, part):
    return head_weight(key, 1)


def draw_w_key(key, part):
    return head_weight(key, 2)


def plant(drawn, stream_key, low, largest):
    spot = [jax.random.randint(jax.random.fold_in(stream_key, axis), (), 0, length) for axis, length in enumerate(drawn.shape)]
    widest = drawn.shape.index(max(drawn.shape))
    next_to = spot[:widest] + [(spot[widest] + 1) % drawn.shape[widest]] + spot[widest + 1:]
    return drawn.at[tuple(spot)].set(low).at[tuple(next_to)].set(largest)


def levels(rng, dims, shards, least, top_value):
    def one(position, parts):
        heights = jax.random.uniform(jax.random.fold_in(jax.random.fold_in(rng, 6), position), (parts,), jnp.float32, least / len(shards), top_value / len(shards))
        return jnp.repeat(jnp.exp(heights), dims[position] // parts).reshape((-1,) + (1,) * (len(dims) - position - 1))

    factor_of = one(*shards[0])
    for cut in shards[1:]:
        factor_of = factor_of * one(*cut)
    return factor_of


def noise(own_key, dims, deviation, reach, split=(), kind=jnp.bfloat16):
    array = jax.random.normal(own_key, dims, jnp.float32) * deviation
    if len(split) > 0:
        array = levels(own_key, dims, split, -0.22, 0.18) * array
    return jnp.clip(array, min=-reach, max=reach).astype(kind)


def setup_inputs(seed: int = 0) -> dict:
    keys = jax.random.split(jax.random.key(seed), 30)
    grid_in = noise(keys[0], (MEMBERS, GRID, F_IN), 1.0, 6.0, ((0, 4), (1, 8)))
    mesh_embed = noise(keys[1], (MESH, D), 1.0, 6.0, ((0, 8),))
    g2m_src = plant(jax.random.randint(keys[2], (BANDS, BANDS, SLOTS), 0, G_DEV), jax.random.fold_in(keys[2], 1), 0, G_DEV - 1).astype(jnp.int32)
    g2m_dst = plant(jax.random.randint(keys[3], (BANDS, BANDS, SLOTS), 0, M_DEV), jax.random.fold_in(keys[3], 1), 0, M_DEV - 1).astype(jnp.int32)
    g2m_own_src = plant(jax.random.randint(keys[4], (BANDS, G2M_OWN), 0, G_DEV), jax.random.fold_in(keys[4], 1), 0, G_DEV - 1).astype(jnp.int32)
    g2m_own_dst = plant(jax.random.randint(keys[5], (BANDS, G2M_OWN), 0, M_DEV), jax.random.fold_in(keys[5], 1), 0, M_DEV - 1).astype(jnp.int32)
    g2m_len = draw_g2m_len(jax.random.fold_in(keys[29], 71), 0)
    mesh_nbr = draw_mesh_nbr(jax.random.fold_in(keys[29], 71), 0)
    halo_rows = plant(jax.random.randint(keys[8], (BANDS, HB), 0, M_DEV), jax.random.fold_in(keys[8], 1), 0, M_DEV - 1).astype(jnp.int32)
    m2g_src = plant(jax.random.randint(keys[9], (BANDS, BANDS, SLOTS), 0, M_DEV), jax.random.fold_in(keys[9], 1), 0, M_DEV - 1).astype(jnp.int32)
    m2g_dst = plant(jax.random.randint(keys[10], (BANDS, BANDS, SLOTS), 0, G_DEV), jax.random.fold_in(keys[10], 1), 0, G_DEV - 1).astype(jnp.int32)
    m2g_own_src = plant(jax.random.randint(keys[11], (BANDS, M2G_OWN), 0, M_DEV), jax.random.fold_in(keys[11], 1), 0, M_DEV - 1).astype(jnp.int32)
    m2g_own_dst = plant(jax.random.randint(keys[12], (BANDS, M2G_OWN), 0, G_DEV), jax.random.fold_in(keys[12], 1), 0, G_DEV - 1).astype(jnp.int32)
    m2g_len = draw_m2g_len(jax.random.fold_in(keys[29], 71), 0)
    w_embed = noise(keys[14], (F_IN, D), F_IN ** -0.5, 0.375)
    w_send = noise(keys[15], (D, D), D ** -0.5, 0.25)
    w_mesh = noise(keys[16], (D, D), D ** -0.5, 0.25)
    attn_gain = jnp.clip(1.0 + 0.18 * jax.random.normal(keys[17], (D,), jnp.float32), 0.1, 1.9)
    w_query = draw_w_query(jax.random.fold_in(keys[29], 71), 0)
    w_key = draw_w_key(jax.random.fold_in(keys[29], 71), 0)
    w_value = noise(keys[20], (D, D), D ** -0.5, 0.25, ((0, 4),))
    w_project = noise(keys[21], (D, D), D ** -0.5, 0.25, ((0, 4),))
    mlp_gain = jnp.clip(1.0 + 0.18 * jax.random.normal(keys[22], (D,), jnp.float32), 0.1, 1.9)
    w_up = noise(keys[23], (D, FFN), D ** -0.5, 0.25, ((0, 4),))
    w_down = noise(keys[24], (FFN, D), FFN ** -0.5, 0.125, ((0, 4),))
    w_return = noise(keys[25], (D, D), D ** -0.5, 0.25)
    w_grid = noise(keys[26], (D, D), D ** -0.5, 0.25)
    w_skip = noise(keys[27], (D, D), D ** -0.5, 0.25)
    w_out = noise(keys[28], (D, F_OUT), D ** -0.5, 0.25)
    return dict(grid_in=grid_in, mesh_embed=mesh_embed, g2m_src=g2m_src, g2m_dst=g2m_dst, g2m_own_src=g2m_own_src, g2m_own_dst=g2m_own_dst, g2m_len=g2m_len, mesh_nbr=mesh_nbr, halo_rows=halo_rows, m2g_src=m2g_src, m2g_dst=m2g_dst, m2g_own_src=m2g_own_src, m2g_own_dst=m2g_own_dst, m2g_len=m2g_len, w_embed=w_embed, w_send=w_send, w_mesh=w_mesh, attn_gain=attn_gain, w_query=w_query, w_key=w_key, w_value=w_value, w_project=w_project, mlp_gain=mlp_gain, w_up=w_up, w_down=w_down, w_return=w_return, w_grid=w_grid, w_skip=w_skip, w_out=w_out)


EPS = 1e-05

def layer_norm(values, norm_gain):
    centred = values - lax.optimization_barrier(jnp.mean(values, axis=-1, keepdims=True))
    spread = lax.optimization_barrier(jnp.mean(centred * centred, axis=-1, keepdims=True))
    return centred * lax.rsqrt(spread + EPS) * norm_gain

def edge_sum(table, src_local, dst_local, own_src, own_dst, lengths, src_rows, dst_rows):
    part_count = src_local.shape[0]
    sender = lax.broadcasted_iota(jnp.int32, src_local.shape, 0)
    target = lax.broadcasted_iota(jnp.int32, src_local.shape, 1)
    column = lax.broadcasted_iota(jnp.int32, src_local.shape, 2)
    source = (sender * src_rows + src_local).reshape(-1)
    landing = target * dst_rows + jnp.transpose(dst_local, (1, 0, 2))
    live_slot = (column < lengths[:, :, None]) & (sender != target)
    landing = jnp.where(live_slot, landing, part_count * dst_rows).reshape(-1)
    band = lax.broadcasted_iota(jnp.int32, own_src.shape, 0)
    own_column = lax.broadcasted_iota(jnp.int32, own_src.shape, 1)
    own_len = jnp.diagonal(lengths)
    own_source = (band * src_rows + own_src).reshape(-1)
    own_landing = jnp.where(own_column < own_len[:, None], band * dst_rows + own_dst, part_count * dst_rows).reshape(-1)
    all_source = jnp.concatenate([source, own_source]).astype(jnp.int32)
    all_landing = jnp.concatenate([landing, own_landing]).astype(jnp.int32)
    carried = table[all_source].astype(jnp.float32)
    summed = jax.ops.segment_sum(carried, all_landing, num_segments=part_count * dst_rows + 1)
    return summed[:part_count * dst_rows]

def attend_block(queries, label_block, key_rows, value_rows):
    block = queries.shape[0]
    slots = K_NBR + 1
    query_heads = queries.reshape(block, H, DH).astype(jnp.float32)
    key_heads = key_rows.reshape(block, slots, H, DH).astype(jnp.float32)
    value_heads = value_rows.reshape(block, slots, H, DH).astype(jnp.float32)
    scores = jnp.einsum('bhd,bkhd->bhk', query_heads, key_heads) / math.sqrt(DH)
    top_score = lax.optimization_barrier(jnp.max(scores, axis=-1, keepdims=True))
    weights = jnp.exp(scores - top_score)
    denom = lax.optimization_barrier(jnp.sum(weights, axis=-1, keepdims=True))
    same = label_block[:, :, None] == label_block[:, None, :]
    repeats = lax.optimization_barrier(jnp.sum(same.astype(jnp.float32), axis=2))
    before = lax.broadcasted_iota(jnp.int32, (1, slots, slots), 2) < lax.broadcasted_iota(jnp.int32, (1, slots, slots), 1)
    first = jnp.logical_not(jnp.any(same & before, axis=2))
    probs = (repeats[:, None, :] * weights / denom).astype(jnp.bfloat16)
    probs = jnp.where(first[:, None, :], probs, jnp.zeros_like(probs))
    mixed = jnp.einsum('bhk,bkhd->bhd', probs.astype(jnp.float32), value_heads)
    return mixed.reshape(block, D).astype(jnp.bfloat16)

def reference(grid_in, mesh_embed, g2m_src, g2m_dst, g2m_own_src, g2m_own_dst, g2m_len, mesh_nbr, halo_rows, m2g_src, m2g_dst, m2g_own_src, m2g_own_dst, m2g_len, w_embed, w_send, w_mesh, attn_gain, w_query, w_key, w_value, w_project, mlp_gain, w_up, w_down, w_return, w_grid, w_skip, w_out):
    halo_global = (jnp.arange(BANDS, dtype=jnp.int32)[:, None] * M_DEV + halo_rows).reshape(-1)
    node_ids = jnp.arange(MESH, dtype=jnp.int32)
    node_part = (node_ids // M_DEV)[:, None]
    remote_pos = jnp.clip(mesh_nbr - M_DEV, 0, BANDS * HB - 1)
    neighbour_global = jnp.where(mesh_nbr < M_DEV, node_part * M_DEV + mesh_nbr, halo_global[remote_pos])
    index_all = jnp.concatenate([node_ids[:, None], neighbour_global], axis=1).astype(jnp.int32)
    label_all = jnp.concatenate([(node_ids % M_DEV)[:, None], mesh_nbr], axis=1).astype(jnp.int32)
    block = min(512, M_DEV)
    count = MESH // block

    def one_member(member_in):
        grid_latent = jax.nn.silu(jnp.dot(member_in, w_embed, preferred_element_type=jnp.float32)).astype(jnp.bfloat16)
        send_rows = jnp.dot(grid_latent, w_send, preferred_element_type=jnp.float32).astype(jnp.bfloat16)
        mesh_agg = edge_sum(send_rows, g2m_src, g2m_dst, g2m_own_src, g2m_own_dst, g2m_len, G_DEV, M_DEV)
        update = jax.nn.silu(jnp.dot(mesh_agg.astype(jnp.bfloat16), w_mesh, preferred_element_type=jnp.float32))
        mesh_state = (mesh_embed.astype(jnp.float32) + update).astype(jnp.bfloat16)
        normed = layer_norm(mesh_state.astype(jnp.float32), attn_gain).astype(jnp.bfloat16)
        queries = jnp.dot(normed, w_query, preferred_element_type=jnp.float32).astype(jnp.bfloat16)
        key_all = jnp.dot(normed, w_key, preferred_element_type=jnp.float32).astype(jnp.bfloat16)
        value_all = jnp.dot(normed, w_value, preferred_element_type=jnp.float32).astype(jnp.bfloat16)

        def run_block(item):
            query_block, index_block, label_block = item
            return attend_block(query_block, label_block, key_all[index_block], value_all[index_block])
        attended = lax.map(run_block, (queries.reshape(count, block, D), index_all.reshape(count, block, K_NBR + 1), label_all.reshape(count, block, K_NBR + 1))).reshape(MESH, D)
        after_attn = mesh_state.astype(jnp.float32) + jnp.dot(attended, w_project, preferred_element_type=jnp.float32)
        normed_two = layer_norm(after_attn, mlp_gain).astype(jnp.bfloat16)
        expanded = jax.nn.silu(jnp.dot(normed_two, w_up, preferred_element_type=jnp.float32)).astype(jnp.bfloat16)
        mesh_out = (after_attn + jnp.dot(expanded, w_down, preferred_element_type=jnp.float32)).astype(jnp.bfloat16)
        return_rows = jnp.dot(mesh_out, w_return, preferred_element_type=jnp.float32).astype(jnp.bfloat16)
        grid_agg = edge_sum(return_rows, m2g_src, m2g_dst, m2g_own_src, m2g_own_dst, m2g_len, M_DEV, G_DEV)
        pre = jnp.dot(grid_agg.astype(jnp.bfloat16), w_grid, preferred_element_type=jnp.float32)
        pre = pre + jnp.dot(grid_latent, w_skip, preferred_element_type=jnp.float32)
        updated = jax.nn.silu(pre).astype(jnp.bfloat16)
        result = lax.dot_general(w_out, updated, (((0,), (1,)), ((), ())), preferred_element_type=jnp.float32)
        return result.astype(jnp.bfloat16)
    return lax.map(one_member, grid_in)
```

```python
import functools
import math

import jax
import jax.numpy as jnp
from jax import lax
from jax.experimental import pallas as pl
from jax.experimental.pallas import tpu as pltpu
from jax.sharding import PartitionSpec as P

DH = 128
EPS = 1e-05
EDGE_BLOCK = 512
BF = jnp.bfloat16
F32 = jnp.float32
MESH = pl.DeviceIdType.MESH


def dot(a, b):
    return jnp.dot(a, b, preferred_element_type=F32)


def dot_nt(a, b):
    return lax.dot_general(a, b, (((1,), (1,)), ((), ())), preferred_element_type=F32)


def silu(v):
    return v / (1.0 + jnp.exp(-v))


def layer_norm(values, norm_gain):
    centred = values - jnp.mean(values, axis=-1, keepdims=True)
    spread = jnp.mean(centred * centred, axis=-1, keepdims=True)
    return centred * lax.rsqrt(spread + EPS) * norm_gain


def iota(shape, dim):
    return lax.broadcasted_iota(jnp.int32, shape, dim)


def one_hot_t(row, rows):
    return jnp.where(iota((rows, row.shape[1]), 0) == row, 1.0, 0.0).astype(BF)


def one_hot(row, rows):
    count = row.shape[1]
    spread = jnp.transpose(jnp.broadcast_to(row, (128, count)))
    lane = iota((count, 128), 1)
    parts = [
        jnp.where(spread == lane + start, 1.0, 0.0).astype(BF) for start in range(0, rows, 128)
    ]
    return jnp.concatenate(parts, axis=1)


def live(row, length, start=0):
    return jnp.where(iota(row.shape, 1) + start < length, row, -1)


def kernel(
    bands, grid_in, mesh_embed, g2m_src, g2m_dst, g2m_own_src, g2m_own_dst, g2m_len, mesh_nbr,
    halo_rows, m2g_src, m2g_dst, m2g_own_src, m2g_own_dst, m2g_len, w_embed, w_send, w_mesh,
    attn_gain, w_query, w_key, w_value, w_project, mlp_gain, w_up, w_down, w_return, w_grid,
    w_skip, w_out, out, attn_w, up_w, down_w, latent, sends, links, links_acc, back, back_acc,
    skip, pick_up, pick_dn, from_lo, from_hi, ret_up, ret_dn, back_lo, back_hi, far,
    wsend, wrecv, msend, mrecv, hsend, hrecv,
):
    me = lax.axis_index("member")
    band = lax.axis_index("space")
    xm = me + 1 - 2 * lax.rem(me, 2)
    ym = lax.rem(me + 2, 4)
    dm = 3 - me
    core = lax.rem(band, 2)
    mate = band + 1 - 2 * core
    has_lower = band > 0
    has_upper = band < bands - 1
    upper = jnp.minimum(band + 1, bands - 1)
    lower = jnp.maximum(band - 1, 0)
    grid_rows = grid_in.shape[1]
    mesh_rows, width = mesh_embed.shape
    hb = halo_rows.shape[1]

    barrier = pltpu.get_barrier_semaphore()
    pl.semaphore_signal(barrier, inc=1, device_id=(xm, band), device_id_type=MESH)
    pl.semaphore_signal(barrier, inc=1, device_id=(ym, band), device_id_type=MESH)
    for off in range(1, bands):
        pl.semaphore_signal(
            barrier, inc=1, device_id=(me, lax.rem(band + off, bands)), device_id_type=MESH
        )
    for i, ref in enumerate((w_query, w_key, w_value, w_project)):
        attn_w[me, i] = ref[...]
    up_w[me] = w_up[...]
    down_w[me] = w_down[...]
    pl.semaphore_wait(barrier, bands + 1)

    def piece(group, slot, part):
        def rows(total):
            half = total // 2
            if part is None:
                return pl.ds(pl.multiple_of(core * half, half), half)
            quarter = half // 2
            return pl.ds(pl.multiple_of(core * half + part * quarter, quarter), quarter)

        if group == 0:
            return attn_w.at[slot, :, rows(attn_w.shape[2])]
        buf = up_w if group == 1 else down_w
        return buf.at[slot, rows(buf.shape[1])]

    def wcopy(group, kind):
        slot, part, target = {
            "a": (me, None, (xm, band)),
            "b": (me, None, (ym, band)),
            "c": (xm, 0, (ym, band)),
            "d": (ym, 1, (xm, band)),
            "e": (xm, None, (me, mate)),
            "f": (ym, None, (me, mate)),
            "g": (dm, None, (me, mate)),
        }[kind]
        k = "abcdefg".index(kind)
        ref = piece(group, slot, part)
        return pltpu.make_async_remote_copy(
            src_ref=ref, dst_ref=ref, send_sem=wsend.at[group, k], recv_sem=wrecv.at[group, k],
            device_id=target, device_id_type=MESH,
        )

    def wstart(group, kinds):
        for kind in kinds:
            wcopy(group, kind).start()

    def wwait(group, kinds):
        for kind in kinds:
            wcopy(group, kind).wait_recv()

    def message(k, src, dst, target):
        return pltpu.make_async_remote_copy(
            src_ref=src, dst_ref=dst, send_sem=msend.at[k], recv_sem=mrecv.at[k],
            device_id=(me, target), device_id_type=MESH,
        )

    wstart(0, "ab")

    block = 256

    def embed(i, carry):
        rows = pl.ds(pl.multiple_of(i * block, block), block)
        lat = silu(dot(grid_in[0, rows, :], w_embed[...])).astype(BF)
        latent[rows, :] = lat
        sends[rows, :] = dot(lat, w_send[...]).astype(BF)
        return carry

    lax.fori_loop(0, grid_rows // block, embed, 0)
    pick_up[...] = dot(one_hot(g2m_src[0, pl.ds(upper, 1), :], grid_rows), sends[...]).astype(BF)
    pick_dn[...] = dot(one_hot(g2m_src[0, pl.ds(lower, 1), :], grid_rows), sends[...]).astype(BF)

    @pl.when(has_upper)
    def _():
        message(0, pick_up, from_lo, upper).start()

    @pl.when(has_lower)
    def _():
        message(1, pick_dn, from_hi, lower).start()

    wwait(0, "ab")
    wstart(0, "cdef")
    wstart(1, "ab")

    links_acc[...] = jnp.zeros_like(links_acc)
    own_length = g2m_len[band, 0]

    def own_links(i, carry):
        start = pl.multiple_of(i * EDGE_BLOCK, EDGE_BLOCK)
        dst = live(g2m_own_dst[:, pl.ds(start, EDGE_BLOCK)], own_length, start)
        src = g2m_own_src[:, pl.ds(start, EDGE_BLOCK)]
        links_acc[...] += dot_nt(one_hot_t(dst, mesh_rows), one_hot_t(src, grid_rows))
        return carry

    lax.fori_loop(0, g2m_own_src.shape[1] // EDGE_BLOCK, own_links, 0)
    links[...] = links_acc[...].astype(BF)
    mesh_agg = dot(links[...], sends[...])

    wwait(0, "cd")
    wstart(0, "g")
    wwait(1, "ab")
    wstart(1, "cdef")
    wstart(2, "ab")

    @pl.when(has_lower)
    def _():
        message(0, pick_up, from_lo, upper).wait_recv()

    @pl.when(has_upper)
    def _():
        message(1, pick_dn, from_hi, lower).wait_recv()

    @pl.when(jnp.logical_not(has_lower))
    def _():
        from_lo[...] = jnp.zeros_like(from_lo)

    @pl.when(jnp.logical_not(has_upper))
    def _():
        from_hi[...] = jnp.zeros_like(from_hi)

    len_lo = jnp.where(has_lower, g2m_len[lower, 0], 0)
    len_hi = jnp.where(has_upper, g2m_len[upper, 0], 0)
    place_lo = one_hot_t(live(g2m_dst[0, pl.ds(lower, 1), :], len_lo), mesh_rows)
    place_hi = one_hot_t(live(g2m_dst[0, pl.ds(upper, 1), :], len_hi), mesh_rows)
    mesh_agg = mesh_agg + dot(place_lo, from_lo[...]) + dot(place_hi, from_hi[...])
    update = silu(dot(mesh_agg.astype(BF), w_mesh[...]))
    mesh_state = (mesh_embed[...].astype(F32) + update).astype(BF)
    normed = layer_norm(mesh_state.astype(F32), attn_gain[...].reshape(1, width)).astype(BF)

    wanted = jnp.zeros((hb, mesh_rows), jnp.int32)
    for j in range(hb):
        wanted = jnp.where(iota((hb, mesh_rows), 0) == j, halo_rows[0, j], wanted)
    picker = jnp.where(wanted == iota((hb, mesh_rows), 1), 1.0, 0.0).astype(BF)
    own_far = pl.ds(pl.multiple_of(band * hb, hb), hb)
    far[own_far, :] = dot(picker, normed).astype(BF)

    def halo(off):
        rows = far.at[own_far]
        return pltpu.make_async_remote_copy(
            src_ref=rows, dst_ref=rows, send_sem=hsend.at[off], recv_sem=hrecv.at[off],
            device_id=(me, lax.rem(band + off, bands)), device_id_type=MESH,
        )

    def halo_in(off):
        rows = far.at[pl.ds(pl.multiple_of(lax.rem(band - off + bands, bands) * hb, hb), hb)]
        return pltpu.make_async_remote_copy(
            src_ref=rows, dst_ref=rows, send_sem=hsend.at[off], recv_sem=hrecv.at[off],
            device_id=(me, lax.rem(band + off, bands)), device_id_type=MESH,
        )

    for off in range(1, bands):
        halo(off).start()

    table = mesh_rows + bands * hb
    nbr = mesh_nbr[...]
    label = iota((mesh_rows, table), 1)
    repeats = jnp.where(label == iota((mesh_rows, table), 0), 1.0, 0.0)
    for k in range(nbr.shape[1]):
        repeats = repeats + jnp.where(nbr[:, k : k + 1] == label, 1.0, 0.0)

    wwait(0, "efg")

    def attn_full(i):
        return attn_w[:, i].reshape(width, width)

    queries = dot(normed, attn_full(0)).astype(BF)
    key_local = dot(normed, attn_full(1)).astype(BF)
    value_local = dot(normed, attn_full(2)).astype(BF)

    wwait(1, "cd")
    wstart(1, "g")
    wwait(2, "ab")
    wstart(2, "cdef")

    for off in range(1, bands):
        halo_in(off).wait_recv()
    keys = jnp.concatenate([key_local, dot(far[...], attn_full(1)).astype(BF)], axis=0)
    values = jnp.concatenate([value_local, dot(far[...], attn_full(2)).astype(BF)], axis=0)
    present = repeats > 0.0
    mixed = []
    for h in range(width // DH):
        cols = slice(h * DH, (h + 1) * DH)
        scores = dot_nt(queries[:, cols], keys[:, cols]) / math.sqrt(DH)
        top = jnp.max(jnp.where(present, scores, -jnp.inf), axis=-1, keepdims=True)
        weights = repeats * jnp.exp(jnp.where(present, scores - top, 0.0))
        probs = (weights / jnp.sum(weights, axis=-1, keepdims=True)).astype(BF)
        mixed.append(dot(probs, values[:, cols]).astype(BF))
    attended = jnp.concatenate(mixed, axis=1)
    after_attn = mesh_state.astype(F32) + dot(attended, attn_full(3))
    normed_two = layer_norm(after_attn, mlp_gain[...].reshape(1, width)).astype(BF)

    wwait(2, "cd")
    wstart(2, "g")

    back_acc[...] = jnp.zeros_like(back_acc)
    back_length = m2g_len[band, 0]

    def own_back(i, carry):
        start = pl.multiple_of(i * EDGE_BLOCK, EDGE_BLOCK)
        dst = live(m2g_own_dst[:, pl.ds(start, EDGE_BLOCK)], back_length, start)
        src = m2g_own_src[:, pl.ds(start, EDGE_BLOCK)]
        back_acc[...] += dot_nt(one_hot_t(dst, grid_rows), one_hot_t(src, mesh_rows))
        return carry

    lax.fori_loop(0, m2g_own_src.shape[1] // EDGE_BLOCK, own_back, 0)
    back[...] = back_acc[...].astype(BF)

    def skip_rows(i, carry):
        rows = pl.ds(pl.multiple_of(i * block, block), block)
        skip[rows, :] = dot(latent[rows, :], w_skip[...])
        return carry

    lax.fori_loop(0, grid_rows // block, skip_rows, 0)

    wwait(1, "efg")
    hidden = down_w.shape[1]
    expanded = []
    for j in range(down_w.shape[0]):
        up = up_w[:, :, j * hidden : (j + 1) * hidden].reshape(width, hidden)
        expanded.append(silu(dot(normed_two, up)).astype(BF))
    wwait(2, "efg")
    total = after_attn
    for j in range(down_w.shape[0]):
        total = total + dot(expanded[j], down_w[j])
    mesh_out = total.astype(BF)
    return_rows = dot(mesh_out, w_return[...]).astype(BF)
    ret_up[...] = dot(one_hot(m2g_src[0, pl.ds(upper, 1), :], mesh_rows), return_rows).astype(BF)
    ret_dn[...] = dot(one_hot(m2g_src[0, pl.ds(lower, 1), :], mesh_rows), return_rows).astype(BF)

    @pl.when(has_upper)
    def _():
        message(2, ret_up, back_lo, upper).start()

    @pl.when(has_lower)
    def _():
        message(3, ret_dn, back_hi, lower).start()

    agg = dot(back[...], return_rows)

    @pl.when(has_lower)
    def _():
        message(2, ret_up, back_lo, upper).wait_recv()

    @pl.when(has_upper)
    def _():
        message(3, ret_dn, back_hi, lower).wait_recv()

    @pl.when(jnp.logical_not(has_lower))
    def _():
        back_lo[...] = jnp.zeros_like(back_lo)

    @pl.when(jnp.logical_not(has_upper))
    def _():
        back_hi[...] = jnp.zeros_like(back_hi)

    blen_lo = jnp.where(has_lower, m2g_len[lower, 0], 0)
    blen_hi = jnp.where(has_upper, m2g_len[upper, 0], 0)
    land_lo = one_hot_t(live(m2g_dst[0, pl.ds(lower, 1), :], blen_lo), grid_rows)
    land_hi = one_hot_t(live(m2g_dst[0, pl.ds(upper, 1), :], blen_hi), grid_rows)
    agg = agg + dot(land_lo, back_lo[...]) + dot(land_hi, back_hi[...])
    pre = dot(agg.astype(BF), w_grid[...]) + skip[...]
    updated = silu(pre).astype(BF)
    f_out = w_out.shape[1]
    padded = jnp.concatenate(
        [w_out[...].astype(F32), jnp.zeros((width, 128 - f_out), F32)], axis=1
    )
    head = jnp.transpose(padded).astype(BF)
    out[...] = dot_nt(head, updated)[:f_out].astype(BF)

    for group in range(3):
        for kind in "abcdefg":
            wcopy(group, kind).wait_send()
    for off in range(1, bands):
        halo(off).wait_send()

    @pl.when(has_upper)
    def _():
        message(0, pick_up, from_lo, upper).wait_send()
        message(2, ret_up, back_lo, upper).wait_send()

    @pl.when(has_lower)
    def _():
        message(1, pick_dn, from_hi, lower).wait_send()
        message(3, ret_dn, back_hi, lower).wait_send()


SCALAR_ARGS = (6, 8, 13)


def shards(*args):
    grid_rows = args[0].shape[1]
    mesh_rows, width = args[1].shape
    slots = args[2].shape[2]
    hb = args[8].shape[1]
    bands = lax.axis_size("space")
    members = lax.axis_size("member")
    depth, ffn = args[23].shape
    down = args[24].shape
    f_out = args[28].shape[1]
    msg = pltpu.VMEM((slots, width), BF)
    in_specs = [
        pl.BlockSpec(memory_space=pltpu.SMEM if i in SCALAR_ARGS else pltpu.VMEM)
        for i in range(len(args))
    ]
    result = pl.pallas_call(
        functools.partial(kernel, bands),
        out_shape=jax.ShapeDtypeStruct((f_out, grid_rows), BF),
        in_specs=in_specs,
        out_specs=pl.BlockSpec(memory_space=pltpu.VMEM),
        scratch_shapes=[
            pltpu.VMEM((members, 4, depth, width), BF),
            pltpu.VMEM((members, depth, ffn), BF),
            pltpu.VMEM((members,) + tuple(down), BF),
            pltpu.VMEM((grid_rows, width), BF),
            pltpu.VMEM((grid_rows, width), BF),
            pltpu.VMEM((mesh_rows, grid_rows), BF),
            pltpu.VMEM((mesh_rows, grid_rows), F32),
            pltpu.VMEM((grid_rows, mesh_rows), BF),
            pltpu.VMEM((grid_rows, mesh_rows), F32),
            pltpu.VMEM((grid_rows, width), F32),
            msg, msg, msg, msg, msg, msg, msg, msg,
            pltpu.VMEM((bands * hb, width), BF),
            pltpu.SemaphoreType.DMA((3, 7)),
            pltpu.SemaphoreType.DMA((3, 7)),
            pltpu.SemaphoreType.DMA((4,)),
            pltpu.SemaphoreType.DMA((4,)),
            pltpu.SemaphoreType.DMA((bands,)),
            pltpu.SemaphoreType.DMA((bands,)),
        ],
        compiler_params=pltpu.CompilerParams(
            collective_id=0, has_side_effects=True, vmem_limit_bytes=52 * 1024 * 1024
        ),
        cost_estimate=pl.CostEstimate(
            flops=8_000_000_000, bytes_accessed=6_000_000, transcendentals=3_000_000
        ),
    )(*args)
    return result[None]


def solution(mesh):
    placed = (
        P("member", "space", None),
        P("space", None),
        P("space", None, None),
        P("space", None, None),
        P("space", None),
        P("space", None),
        P(None, "space"),
        P("space", None),
        P("space", None),
        P("space", None, None),
        P("space", None, None),
        P("space", None),
        P("space", None),
        P(None, "space"),
        P(),
        P(),
        P(),
        P(),
        P("member", None),
        P("member", None),
        P("member", None),
        P("member", None),
        P(),
        P("member", None),
        P("member", None),
        P(),
        P(),
        P(),
        P(),
    )
    return jax.shard_map(
        shards, mesh=mesh, in_specs=placed, out_specs=P("member", None, "space"), check_vma=False
    )
```

```python
import functools
import math

import jax
import jax.numpy as jnp
from jax import lax
from jax.experimental import pallas as pl
from jax.experimental.pallas import tpu as pltpu
from jax.sharding import PartitionSpec as P

DH = 128
EPS = 1e-05
EDGE_BLOCK = 512
BF = jnp.bfloat16
F32 = jnp.float32
MESH = pl.DeviceIdType.MESH


def dot(a, b):
    return jnp.dot(a, b, preferred_element_type=F32)


def dot_nt(a, b):
    return lax.dot_general(a, b, (((1,), (1,)), ((), ())), preferred_element_type=F32)


def silu(v):
    return v / (1.0 + jnp.exp(-v))


def layer_norm(values, norm_gain):
    centred = values - jnp.mean(values, axis=-1, keepdims=True)
    spread = jnp.mean(centred * centred, axis=-1, keepdims=True)
    return centred * lax.rsqrt(spread + EPS) * norm_gain


def iota(shape, dim):
    return lax.broadcasted_iota(jnp.int32, shape, dim)


def one_hot_t(row, rows):
    return jnp.where(iota((rows, row.shape[1]), 0) == row, 1.0, 0.0).astype(BF)


def one_hot(row, rows):
    count = row.shape[1]
    spread = jnp.transpose(jnp.broadcast_to(row, (128, count)))
    lane = iota((count, 128), 1)
    parts = [
        jnp.where(spread == lane + start, 1.0, 0.0).astype(BF) for start in range(0, rows, 128)
    ]
    return jnp.concatenate(parts, axis=1)


def live(row, length, start=0):
    return jnp.where(iota(row.shape, 1) + start < length, row, -1)


def kernel(bands, *refs):
    hbm = dict(zip(NAMES, refs))
    head = refs[len(NAMES) - 1]
    out = refs[len(NAMES)]
    rest = refs[len(NAMES) + 1 :]
    stage = dict(zip(STAGED, rest))
    (
        attn_w, up_w, down_w, latent, sends, links, links_acc, back, back_acc,
        skip, pick_up, pick_dn, from_lo, from_hi, ret_up, ret_dn, back_lo, back_hi, far,
        expanded, wsend, wrecv, msend, mrecv, hsend, hrecv, fetched,
    ) = rest[len(STAGED) :]
    grid_in, mesh_embed, g2m_src, g2m_dst = (stage[n] for n in STAGED[:4])
    g2m_own_src, g2m_own_dst, g2m_len, mesh_nbr = (stage[n] for n in STAGED[4:8])
    halo_rows, m2g_src, m2g_dst, m2g_own_src = (stage[n] for n in STAGED[8:12])
    m2g_own_dst, m2g_len, w_embed, w_send = (stage[n] for n in STAGED[12:16])
    w_mesh, attn_gain, mlp_gain, w_return = (stage[n] for n in STAGED[16:20])
    w_grid, w_skip = (stage[n] for n in STAGED[20:])
    me = lax.axis_index("member")
    band = lax.axis_index("space")
    xm = me + 1 - 2 * lax.rem(me, 2)
    ym = lax.rem(me + 2, 4)
    dm = 3 - me
    core = lax.rem(band, 2)
    mate = band + 1 - 2 * core
    has_lower = band > 0
    has_upper = band < bands - 1
    upper = jnp.minimum(band + 1, bands - 1)
    lower = jnp.maximum(band - 1, 0)
    grid_rows = grid_in.shape[1]
    mesh_rows, width = mesh_embed.shape
    hb = halo_rows.shape[1]

    barrier = pltpu.get_barrier_semaphore()
    pl.semaphore_signal(barrier, inc=1, device_id=(xm, band), device_id_type=MESH)
    pl.semaphore_signal(barrier, inc=1, device_id=(ym, band), device_id_type=MESH)
    for off in range(1, bands):
        pl.semaphore_signal(
            barrier, inc=1, device_id=(me, lax.rem(band + off, bands)), device_id_type=MESH
        )
    homes = {
        "w_query": attn_w.at[me, 0], "w_key": attn_w.at[me, 1], "w_value": attn_w.at[me, 2],
        "w_project": attn_w.at[me, 3], "w_up": up_w.at[me], "w_down": down_w.at[me],
    }

    def fetch(name):
        target = homes[name] if name in homes else stage[name]
        return pltpu.make_async_copy(hbm[name], target, fetched.at[NAMES.index(name)])

    def ready(*names):
        for name in names:
            fetch(name).wait()

    for name in FETCH_ORDER:
        fetch(name).start()
    pl.semaphore_wait(barrier, bands + 1)
    ready("w_query", "w_key", "w_value", "w_project")

    def piece(group, slot, part):
        def rows(total):
            half = total // 2
            if part is None:
                return pl.ds(pl.multiple_of(core * half, half), half)
            quarter = half // 2
            return pl.ds(pl.multiple_of(core * half + part * quarter, quarter), quarter)

        if group == 0:
            return attn_w.at[slot, :, rows(attn_w.shape[2])]
        buf = up_w if group == 1 else down_w
        return buf.at[slot, rows(buf.shape[1])]

    def wcopy(group, kind):
        slot, part, target = {
            "a": (me, None, (xm, band)),
            "b": (me, None, (ym, band)),
            "c": (xm, 0, (ym, band)),
            "d": (ym, 1, (xm, band)),
            "e": (xm, None, (me, mate)),
            "f": (ym, None, (me, mate)),
            "g": (dm, None, (me, mate)),
        }[kind]
        k = "abcdefg".index(kind)
        ref = piece(group, slot, part)
        return pltpu.make_async_remote_copy(
            src_ref=ref, dst_ref=ref, send_sem=wsend.at[group, k], recv_sem=wrecv.at[group, k],
            device_id=target, device_id_type=MESH,
        )

    def wstart(group, kinds):
        for kind in kinds:
            wcopy(group, kind).start()

    def wwait(group, kinds):
        for kind in kinds:
            wcopy(group, kind).wait_recv()

    def message(k, src, dst, target):
        return pltpu.make_async_remote_copy(
            src_ref=src, dst_ref=dst, send_sem=msend.at[k], recv_sem=mrecv.at[k],
            device_id=(me, target), device_id_type=MESH,
        )

    wstart(0, "ab")

    ready("grid_in", "w_embed", "w_send", "g2m_src")

    block = 256

    def embed(i, carry):
        rows = pl.ds(pl.multiple_of(i * block, block), block)
        lat = silu(dot(grid_in[0, rows, :], w_embed[...])).astype(BF)
        latent[rows, :] = lat
        sends[rows, :] = dot(lat, w_send[...]).astype(BF)
        return carry

    lax.fori_loop(0, grid_rows // block, embed, 0)
    pick_up[...] = dot(one_hot(g2m_src[0, pl.ds(upper, 1), :], grid_rows), sends[...]).astype(BF)
    pick_dn[...] = dot(one_hot(g2m_src[0, pl.ds(lower, 1), :], grid_rows), sends[...]).astype(BF)

    @pl.when(has_upper)
    def _():
        message(0, pick_up, from_lo, upper).start()

    @pl.when(has_lower)
    def _():
        message(1, pick_dn, from_hi, lower).start()

    wwait(0, "ab")
    wstart(0, "cdef")
    ready("w_up", "w_down")
    wstart(1, "ab")
    ready("g2m_len", "g2m_own_src", "g2m_own_dst", "g2m_dst", "w_mesh", "mesh_embed")
    ready("attn_gain", "halo_rows", "mesh_nbr", "m2g_len", "m2g_own_src", "m2g_own_dst")
    ready("mlp_gain", "m2g_src", "m2g_dst", "w_skip", "w_return", "w_grid")

    links_acc[...] = jnp.zeros_like(links_acc)
    own_length = g2m_len[0, band]

    def own_links(i, carry):
        start = pl.multiple_of(i * EDGE_BLOCK, EDGE_BLOCK)
        dst = live(g2m_own_dst[:, pl.ds(start, EDGE_BLOCK)], own_length, start)
        src = g2m_own_src[:, pl.ds(start, EDGE_BLOCK)]
        links_acc[...] += dot_nt(one_hot_t(dst, mesh_rows), one_hot_t(src, grid_rows))
        return carry

    lax.fori_loop(0, g2m_own_src.shape[1] // EDGE_BLOCK, own_links, 0)
    links[...] = links_acc[...].astype(BF)
    mesh_agg = dot(links[...], sends[...])

    wwait(0, "cd")
    wstart(0, "g")

    @pl.when(has_lower)
    def _():
        message(0, pick_up, from_lo, upper).wait_recv()

    @pl.when(has_upper)
    def _():
        message(1, pick_dn, from_hi, lower).wait_recv()

    @pl.when(jnp.logical_not(has_lower))
    def _():
        from_lo[...] = jnp.zeros_like(from_lo)

    @pl.when(jnp.logical_not(has_upper))
    def _():
        from_hi[...] = jnp.zeros_like(from_hi)

    len_lo = jnp.where(has_lower, g2m_len[0, lower], 0)
    len_hi = jnp.where(has_upper, g2m_len[0, upper], 0)
    place_lo = one_hot_t(live(g2m_dst[0, pl.ds(lower, 1), :], len_lo), mesh_rows)
    place_hi = one_hot_t(live(g2m_dst[0, pl.ds(upper, 1), :], len_hi), mesh_rows)
    mesh_agg = mesh_agg + dot(place_lo, from_lo[...]) + dot(place_hi, from_hi[...])
    update = silu(dot(mesh_agg.astype(BF), w_mesh[...]))
    mesh_state = (mesh_embed[...].astype(F32) + update).astype(BF)
    normed = layer_norm(mesh_state.astype(F32), attn_gain[...]).astype(BF)

    wanted = jnp.zeros((hb, mesh_rows), jnp.int32)
    for j in range(hb):
        wanted = jnp.where(iota((hb, mesh_rows), 0) == j, halo_rows[0, j], wanted)
    picker = jnp.where(wanted == iota((hb, mesh_rows), 1), 1.0, 0.0).astype(BF)
    own_far = pl.ds(pl.multiple_of(band * hb, hb), hb)
    far[own_far, :] = dot(picker, normed).astype(BF)

    def halo(off):
        rows = far.at[own_far]
        return pltpu.make_async_remote_copy(
            src_ref=rows, dst_ref=rows, send_sem=hsend.at[off], recv_sem=hrecv.at[off],
            device_id=(me, lax.rem(band + off, bands)), device_id_type=MESH,
        )

    def halo_in(off):
        rows = far.at[pl.ds(pl.multiple_of(lax.rem(band - off + bands, bands) * hb, hb), hb)]
        return pltpu.make_async_remote_copy(
            src_ref=rows, dst_ref=rows, send_sem=hsend.at[off], recv_sem=hrecv.at[off],
            device_id=(me, lax.rem(band + off, bands)), device_id_type=MESH,
        )

    for off in range(1, bands):
        halo(off).start()

    wwait(1, "ab")
    wstart(1, "cdef")
    wstart(2, "ab")

    table = mesh_rows + bands * hb
    label = iota((table, mesh_rows), 0)
    repeats = jnp.where(label == iota((table, mesh_rows), 1), 1.0, 0.0)
    for k in range(mesh_nbr.shape[0]):
        repeats = repeats + jnp.where(mesh_nbr[k : k + 1, :] == label, 1.0, 0.0)
    repeats = jnp.transpose(repeats)

    wwait(0, "efg")

    def attn_full(i):
        return attn_w[:, i].reshape(width, width)

    queries = dot(normed, attn_full(0)).astype(BF)
    key_local = dot(normed, attn_full(1)).astype(BF)
    value_local = dot(normed, attn_full(2)).astype(BF)

    for off in range(1, bands):
        halo_in(off).wait_recv()
    keys = jnp.concatenate([key_local, dot(far[...], attn_full(1)).astype(BF)], axis=0)
    values = jnp.concatenate([value_local, dot(far[...], attn_full(2)).astype(BF)], axis=0)
    present = repeats > 0.0
    mixed = []
    for h in range(width // DH):
        cols = slice(h * DH, (h + 1) * DH)
        scores = dot_nt(queries[:, cols], keys[:, cols]) / math.sqrt(DH)
        top = jnp.max(jnp.where(present, scores, -jnp.inf), axis=-1, keepdims=True)
        weights = repeats * jnp.exp(jnp.where(present, scores - top, 0.0))
        probs = (weights / jnp.sum(weights, axis=-1, keepdims=True)).astype(BF)
        mixed.append(dot(probs, values[:, cols]).astype(BF))
    attended = jnp.concatenate(mixed, axis=1)
    after_attn = mesh_state.astype(F32) + dot(attended, attn_full(3))
    normed_two = layer_norm(after_attn, mlp_gain[...]).astype(BF)

    wwait(1, "cd")
    wstart(1, "g")
    wwait(2, "ab")
    wstart(2, "cdef")

    back_acc[...] = jnp.zeros_like(back_acc)
    back_length = m2g_len[0, band]

    def own_back(i, carry):
        start = pl.multiple_of(i * EDGE_BLOCK, EDGE_BLOCK)
        dst = live(m2g_own_dst[:, pl.ds(start, EDGE_BLOCK)], back_length, start)
        src = m2g_own_src[:, pl.ds(start, EDGE_BLOCK)]
        back_acc[...] += dot_nt(one_hot_t(dst, grid_rows), one_hot_t(src, mesh_rows))
        return carry

    lax.fori_loop(0, m2g_own_src.shape[1] // EDGE_BLOCK, own_back, 0)
    back[...] = back_acc[...].astype(BF)

    wwait(2, "cd")
    wstart(2, "g")

    wwait(1, "efg")
    hidden = down_w.shape[1]
    for j in range(down_w.shape[0]):
        up = up_w[:, :, j * hidden : (j + 1) * hidden].reshape(width, hidden)
        expanded[j] = silu(dot(normed_two, up)).astype(BF)
    total = after_attn + dot(expanded[me], down_w[me])
    for kind, slot in (("e", xm), ("f", ym), ("g", dm)):
        wwait(2, kind)
        total = total + dot(expanded[slot], down_w[slot])
    mesh_out = total.astype(BF)
    return_rows = dot(mesh_out, w_return[...]).astype(BF)
    ret_up[...] = dot(one_hot(m2g_src[0, pl.ds(upper, 1), :], mesh_rows), return_rows).astype(BF)
    ret_dn[...] = dot(one_hot(m2g_src[0, pl.ds(lower, 1), :], mesh_rows), return_rows).astype(BF)

    @pl.when(has_upper)
    def _():
        message(2, ret_up, back_lo, upper).start()

    @pl.when(has_lower)
    def _():
        message(3, ret_dn, back_hi, lower).start()

    def skip_rows(i, carry):
        rows = pl.ds(pl.multiple_of(i * block, block), block)
        skip[rows, :] = dot(latent[rows, :], w_skip[...])
        return carry

    lax.fori_loop(0, grid_rows // block, skip_rows, 0)
    agg = dot(back[...], return_rows)
    blen_lo = jnp.where(has_lower, m2g_len[0, lower], 0)
    blen_hi = jnp.where(has_upper, m2g_len[0, upper], 0)
    land_lo = one_hot_t(live(m2g_dst[0, pl.ds(lower, 1), :], blen_lo), grid_rows)
    land_hi = one_hot_t(live(m2g_dst[0, pl.ds(upper, 1), :], blen_hi), grid_rows)

    @pl.when(has_lower)
    def _():
        message(2, ret_up, back_lo, upper).wait_recv()

    @pl.when(has_upper)
    def _():
        message(3, ret_dn, back_hi, lower).wait_recv()

    @pl.when(jnp.logical_not(has_lower))
    def _():
        back_lo[...] = jnp.zeros_like(back_lo)

    @pl.when(jnp.logical_not(has_upper))
    def _():
        back_hi[...] = jnp.zeros_like(back_hi)

    agg = agg + dot(land_lo, back_lo[...]) + dot(land_hi, back_hi[...])
    pre = dot(agg.astype(BF), w_grid[...]) + skip[...]
    updated = silu(pre).astype(BF)
    out[...] = dot_nt(head[...], updated).astype(BF)

    for group in range(3):
        for kind in "abcdefg":
            wcopy(group, kind).wait_send()
    for off in range(1, bands):
        halo(off).wait_send()

    @pl.when(has_upper)
    def _():
        message(0, pick_up, from_lo, upper).wait_send()
        message(2, ret_up, back_lo, upper).wait_send()

    @pl.when(has_lower)
    def _():
        message(1, pick_dn, from_hi, lower).wait_send()
        message(3, ret_dn, back_hi, lower).wait_send()


NAMES = (
    "grid_in", "mesh_embed", "g2m_src", "g2m_dst", "g2m_own_src", "g2m_own_dst", "g2m_len",
    "mesh_nbr", "halo_rows", "m2g_src", "m2g_dst", "m2g_own_src", "m2g_own_dst", "m2g_len",
    "w_embed", "w_send", "w_mesh", "attn_gain", "w_query", "w_key", "w_value", "w_project",
    "mlp_gain", "w_up", "w_down", "w_return", "w_grid", "w_skip", "w_out",
)
SHARDED = ("w_query", "w_key", "w_value", "w_project", "w_up", "w_down")
STAGED = tuple(n for n in NAMES[:-1] if n not in SHARDED)
SCALARS = ("g2m_len", "halo_rows", "m2g_len")
FIRST = ("w_query", "w_key", "w_value", "w_project", "grid_in", "w_embed", "w_send", "g2m_src")
FETCH_ORDER = FIRST + ("w_up", "w_down") + tuple(
    n for n in STAGED if n not in FIRST
)


def shards(*args):
    args = list(args)
    for name in ("g2m_len", "m2g_len", "mesh_nbr", "w_out"):
        i = NAMES.index(name)
        args[i] = args[i].T
    for name in ("attn_gain", "mlp_gain"):
        i = NAMES.index(name)
        args[i] = args[i].reshape(1, -1)
    grid_rows = args[0].shape[1]
    mesh_rows, width = args[1].shape
    slots = args[2].shape[2]
    hb = args[8].shape[1]
    bands = lax.axis_size("space")
    members = lax.axis_size("member")
    depth, ffn = args[23].shape
    down = args[24].shape
    f_out = args[28].shape[0]
    named = dict(zip(NAMES, args))
    staging = [
        (pltpu.SMEM if n in SCALARS else pltpu.VMEM)(named[n].shape, named[n].dtype)
        for n in STAGED
    ]
    msg = pltpu.VMEM((slots, width), BF)
    in_specs = [pl.BlockSpec(memory_space=pltpu.HBM)] * (len(args) - 1)
    in_specs.append(pl.BlockSpec(memory_space=pltpu.VMEM))
    result = pl.pallas_call(
        functools.partial(kernel, bands),
        out_shape=jax.ShapeDtypeStruct((f_out, grid_rows), BF),
        in_specs=in_specs,
        out_specs=pl.BlockSpec(memory_space=pltpu.VMEM),
        scratch_shapes=staging + [
            pltpu.VMEM((members, 4, depth, width), BF),
            pltpu.VMEM((members, depth, ffn), BF),
            pltpu.VMEM((members,) + tuple(down), BF),
            pltpu.VMEM((grid_rows, width), BF),
            pltpu.VMEM((grid_rows, width), BF),
            pltpu.VMEM((mesh_rows, grid_rows), BF),
            pltpu.VMEM((mesh_rows, grid_rows), F32),
            pltpu.VMEM((grid_rows, mesh_rows), BF),
            pltpu.VMEM((grid_rows, mesh_rows), F32),
            pltpu.VMEM((grid_rows, width), F32),
            msg, msg, msg, msg, msg, msg, msg, msg,
            pltpu.VMEM((bands * hb, width), BF),
            pltpu.VMEM((members, mesh_rows, down[0]), BF),
            pltpu.SemaphoreType.DMA((3, 7)),
            pltpu.SemaphoreType.DMA((3, 7)),
            pltpu.SemaphoreType.DMA((4,)),
            pltpu.SemaphoreType.DMA((4,)),
            pltpu.SemaphoreType.DMA((bands,)),
            pltpu.SemaphoreType.DMA((bands,)),
            pltpu.SemaphoreType.DMA((len(NAMES),)),
        ],
        compiler_params=pltpu.CompilerParams(
            collective_id=0, has_side_effects=True, vmem_limit_bytes=66060288
        ),
        cost_estimate=pl.CostEstimate(
            flops=8_000_000_000, bytes_accessed=6_000_000, transcendentals=3_000_000
        ),
    )(*args)
    return result[None]


def solution(mesh):
    placed = (
        P("member", "space", None),
        P("space", None),
        P("space", None, None),
        P("space", None, None),
        P("space", None),
        P("space", None),
        P(None, "space"),
        P("space", None),
        P("space", None),
        P("space", None, None),
        P("space", None, None),
        P("space", None),
        P("space", None),
        P(None, "space"),
        P(),
        P(),
        P(),
        P(),
        P("member", None),
        P("member", None),
        P("member", None),
        P("member", None),
        P(),
        P("member", None),
        P("member", None),
        P(),
        P(),
        P(),
        P(),
    )
    return jax.shard_map(
        shards, mesh=mesh, in_specs=placed, out_specs=P("member", None, "space"), check_vma=False
    )
```

```python
import functools
import math

import jax
import jax.numpy as jnp
from jax import lax
from jax.experimental import pallas as pl
from jax.experimental.pallas import tpu as pltpu
from jax.sharding import PartitionSpec as P

DH = 128
EPS = 1e-05
EDGE_BLOCK = 512
BF = jnp.bfloat16
F32 = jnp.float32
MESH = pl.DeviceIdType.MESH


def dot(a, b):
    return jnp.dot(a, b, preferred_element_type=F32)


def dot_nt(a, b):
    return lax.dot_general(a, b, (((1,), (1,)), ((), ())), preferred_element_type=F32)


def silu(v):
    return v / (1.0 + jnp.exp(-v))


def layer_norm(values, norm_gain):
    centred = values - jnp.mean(values, axis=-1, keepdims=True)
    spread = jnp.mean(centred * centred, axis=-1, keepdims=True)
    return centred * lax.rsqrt(spread + EPS) * norm_gain


def iota(shape, dim):
    return lax.broadcasted_iota(jnp.int32, shape, dim)


def one_hot_t(row, rows):
    return jnp.where(iota((rows, row.shape[1]), 0) == row, 1.0, 0.0).astype(BF)


def one_hot(row, rows):
    count = row.shape[1]
    spread = jnp.transpose(jnp.broadcast_to(row, (128, count)))
    lane = iota((count, 128), 1)
    parts = [
        jnp.where(spread == lane + start, 1.0, 0.0).astype(BF) for start in range(0, rows, 128)
    ]
    return jnp.concatenate(parts, axis=1)


def live(row, length, start=0):
    return jnp.where(iota(row.shape, 1) + start < length, row, -1)


def kernel(bands, *refs):
    hbm = dict(zip(NAMES, refs))
    head = refs[len(NAMES) - 1]
    out = refs[len(NAMES)]
    rest = refs[len(NAMES) + 1 :]
    stage = dict(zip(STAGED, rest))
    (
        attn_w, up_w, down_w, latent, sends, links, links_acc, back, back_acc,
        skip, pick_up, pick_dn, from_lo, from_hi, ret_up, ret_dn, back_lo, back_hi, far,
        expanded, wsend, wrecv, msend, mrecv, hsend, hrecv, fetched,
    ) = rest[len(STAGED) :]
    grid_in, mesh_embed, g2m_src, g2m_dst = (stage[n] for n in STAGED[:4])
    g2m_own_src, g2m_own_dst, g2m_len, mesh_nbr = (stage[n] for n in STAGED[4:8])
    halo_rows, m2g_src, m2g_dst, m2g_own_src = (stage[n] for n in STAGED[8:12])
    m2g_own_dst, m2g_len, w_embed, w_send = (stage[n] for n in STAGED[12:16])
    w_mesh, attn_gain, mlp_gain, w_return = (stage[n] for n in STAGED[16:20])
    w_grid, w_skip = (stage[n] for n in STAGED[20:])
    me = lax.axis_index("member")
    band = lax.axis_index("space")
    xm = me + 1 - 2 * lax.rem(me, 2)
    ym = lax.rem(me + 2, 4)
    dm = 3 - me
    core = lax.rem(band, 2)
    mate = band + 1 - 2 * core
    has_lower = band > 0
    has_upper = band < bands - 1
    upper = jnp.minimum(band + 1, bands - 1)
    lower = jnp.maximum(band - 1, 0)
    grid_rows = grid_in.shape[1]
    mesh_rows, width = mesh_embed.shape
    hb = halo_rows.shape[1]

    barrier = pltpu.get_barrier_semaphore()
    pl.semaphore_signal(barrier, inc=1, device_id=(xm, band), device_id_type=MESH)
    pl.semaphore_signal(barrier, inc=1, device_id=(ym, band), device_id_type=MESH)
    for off in range(1, bands):
        pl.semaphore_signal(
            barrier, inc=1, device_id=(me, lax.rem(band + off, bands)), device_id_type=MESH
        )
    homes = {
        "w_query": attn_w.at[me, 0], "w_key": attn_w.at[me, 1], "w_value": attn_w.at[me, 2],
        "w_project": attn_w.at[me, 3], "w_up": up_w.at[me], "w_down": down_w.at[me],
    }

    def fetch(name):
        target = homes[name] if name in homes else stage[name]
        return pltpu.make_async_copy(hbm[name], target, fetched.at[NAMES.index(name)])

    def ready(*names):
        for name in names:
            fetch(name).wait()

    for name in FETCH_ORDER:
        fetch(name).start()
    pl.semaphore_wait(barrier, bands + 1)
    ready("w_query", "w_key", "w_value", "w_project")

    def piece(group, slot, part):
        def rows(total):
            half = total // 2
            if part is None:
                return pl.ds(pl.multiple_of(core * half, half), half)
            quarter = half // 2
            return pl.ds(pl.multiple_of(core * half + part * quarter, quarter), quarter)

        if group == 0:
            return attn_w.at[slot, :, rows(attn_w.shape[2])]
        buf = up_w if group == 1 else down_w
        return buf.at[slot, rows(buf.shape[1])]

    def wcopy(group, kind):
        slot, part, target = {
            "a": (me, None, (xm, band)),
            "b": (me, None, (ym, band)),
            "c": (xm, 0, (ym, band)),
            "d": (ym, 1, (xm, band)),
            "e": (xm, None, (me, mate)),
            "f": (ym, None, (me, mate)),
            "g": (dm, None, (me, mate)),
        }[kind]
        k = "abcdefg".index(kind)
        ref = piece(group, slot, part)
        return pltpu.make_async_remote_copy(
            src_ref=ref, dst_ref=ref, send_sem=wsend.at[group, k], recv_sem=wrecv.at[group, k],
            device_id=target, device_id_type=MESH,
        )

    def wstart(group, kinds):
        for kind in kinds:
            wcopy(group, kind).start()

    def wwait(group, kinds):
        for kind in kinds:
            wcopy(group, kind).wait_recv()

    def message(k, src, dst, target):
        return pltpu.make_async_remote_copy(
            src_ref=src, dst_ref=dst, send_sem=msend.at[k], recv_sem=mrecv.at[k],
            device_id=(me, target), device_id_type=MESH,
        )

    wstart(0, "ab")
    ready("w_up", "w_down")
    wstart(1, "ab")

    ready("grid_in", "w_embed", "w_send", "g2m_src")

    block = 256

    def embed(i, carry):
        rows = pl.ds(pl.multiple_of(i * block, block), block)
        lat = silu(dot(grid_in[0, rows, :], w_embed[...])).astype(BF)
        latent[rows, :] = lat
        sends[rows, :] = dot(lat, w_send[...]).astype(BF)
        return carry

    lax.fori_loop(0, grid_rows // block, embed, 0)
    pick_up[...] = dot(one_hot(g2m_src[0, pl.ds(upper, 1), :], grid_rows), sends[...]).astype(BF)
    pick_dn[...] = dot(one_hot(g2m_src[0, pl.ds(lower, 1), :], grid_rows), sends[...]).astype(BF)

    @pl.when(has_upper)
    def _():
        message(0, pick_up, from_lo, upper).start()

    @pl.when(has_lower)
    def _():
        message(1, pick_dn, from_hi, lower).start()

    wwait(0, "ab")
    wstart(0, "cdef")
    wstart(2, "ab")
    ready("g2m_len", "g2m_own_src", "g2m_own_dst", "g2m_dst", "w_mesh", "mesh_embed")
    ready("attn_gain", "halo_rows", "mesh_nbr", "m2g_len", "m2g_own_src", "m2g_own_dst")
    ready("mlp_gain", "m2g_src", "m2g_dst", "w_skip", "w_return", "w_grid")

    links_acc[...] = jnp.zeros_like(links_acc)
    own_length = g2m_len[0, band]

    def own_links(i, carry):
        start = pl.multiple_of(i * EDGE_BLOCK, EDGE_BLOCK)
        dst = live(g2m_own_dst[:, pl.ds(start, EDGE_BLOCK)], own_length, start)
        src = g2m_own_src[:, pl.ds(start, EDGE_BLOCK)]
        links_acc[...] += dot_nt(one_hot_t(dst, mesh_rows), one_hot_t(src, grid_rows))
        return carry

    lax.fori_loop(0, g2m_own_src.shape[1] // EDGE_BLOCK, own_links, 0)
    links[...] = links_acc[...].astype(BF)
    mesh_agg = dot(links[...], sends[...])

    wwait(0, "cd")
    wstart(0, "g")

    @pl.when(has_lower)
    def _():
        message(0, pick_up, from_lo, upper).wait_recv()

    @pl.when(has_upper)
    def _():
        message(1, pick_dn, from_hi, lower).wait_recv()

    @pl.when(jnp.logical_not(has_lower))
    def _():
        from_lo[...] = jnp.zeros_like(from_lo)

    @pl.when(jnp.logical_not(has_upper))
    def _():
        from_hi[...] = jnp.zeros_like(from_hi)

    len_lo = jnp.where(has_lower, g2m_len[0, lower], 0)
    len_hi = jnp.where(has_upper, g2m_len[0, upper], 0)
    place_lo = one_hot_t(live(g2m_dst[0, pl.ds(lower, 1), :], len_lo), mesh_rows)
    place_hi = one_hot_t(live(g2m_dst[0, pl.ds(upper, 1), :], len_hi), mesh_rows)
    mesh_agg = mesh_agg + dot(place_lo, from_lo[...]) + dot(place_hi, from_hi[...])
    update = silu(dot(mesh_agg.astype(BF), w_mesh[...]))
    mesh_state = (mesh_embed[...].astype(F32) + update).astype(BF)
    normed = layer_norm(mesh_state.astype(F32), attn_gain[...]).astype(BF)

    wanted = jnp.zeros((hb, mesh_rows), jnp.int32)
    for j in range(hb):
        wanted = jnp.where(iota((hb, mesh_rows), 0) == j, halo_rows[0, j], wanted)
    picker = jnp.where(wanted == iota((hb, mesh_rows), 1), 1.0, 0.0).astype(BF)
    own_far = pl.ds(pl.multiple_of(band * hb, hb), hb)
    far[own_far, :] = dot(picker, normed).astype(BF)

    def halo(off):
        rows = far.at[own_far]
        return pltpu.make_async_remote_copy(
            src_ref=rows, dst_ref=rows, send_sem=hsend.at[off], recv_sem=hrecv.at[off],
            device_id=(me, lax.rem(band + off, bands)), device_id_type=MESH,
        )

    def halo_in(off):
        rows = far.at[pl.ds(pl.multiple_of(lax.rem(band - off + bands, bands) * hb, hb), hb)]
        return pltpu.make_async_remote_copy(
            src_ref=rows, dst_ref=rows, send_sem=hsend.at[off], recv_sem=hrecv.at[off],
            device_id=(me, lax.rem(band + off, bands)), device_id_type=MESH,
        )

    for off in range(1, bands):
        halo(off).start()

    wwait(1, "ab")
    wstart(1, "cdef")

    table = mesh_rows + bands * hb
    label = iota((table, mesh_rows), 0)
    repeats = jnp.where(label == iota((table, mesh_rows), 1), 1.0, 0.0)
    for k in range(mesh_nbr.shape[0]):
        repeats = repeats + jnp.where(mesh_nbr[k : k + 1, :] == label, 1.0, 0.0)
    repeats = jnp.transpose(repeats)

    wwait(0, "efg")

    def attn_full(i):
        return attn_w[:, i].reshape(width, width)

    queries = dot(normed, attn_full(0)).astype(BF)
    key_local = dot(normed, attn_full(1)).astype(BF)
    value_local = dot(normed, attn_full(2)).astype(BF)

    for off in range(1, bands):
        halo_in(off).wait_recv()
    keys = jnp.concatenate([key_local, dot(far[...], attn_full(1)).astype(BF)], axis=0)
    values = jnp.concatenate([value_local, dot(far[...], attn_full(2)).astype(BF)], axis=0)
    present = repeats > 0.0
    mixed = []
    for h in range(width // DH):
        cols = slice(h * DH, (h + 1) * DH)
        scores = dot_nt(queries[:, cols], keys[:, cols]) / math.sqrt(DH)
        top = jnp.max(jnp.where(present, scores, -jnp.inf), axis=-1, keepdims=True)
        weights = repeats * jnp.exp(jnp.where(present, scores - top, 0.0))
        probs = (weights / jnp.sum(weights, axis=-1, keepdims=True)).astype(BF)
        mixed.append(dot(probs, values[:, cols]).astype(BF))
    attended = jnp.concatenate(mixed, axis=1)
    after_attn = mesh_state.astype(F32) + dot(attended, attn_full(3))
    normed_two = layer_norm(after_attn, mlp_gain[...]).astype(BF)

    wwait(1, "cd")
    wstart(1, "g")
    wwait(2, "ab")
    wstart(2, "cdef")

    back_acc[...] = jnp.zeros_like(back_acc)
    back_length = m2g_len[0, band]

    def own_back(i, carry):
        start = pl.multiple_of(i * EDGE_BLOCK, EDGE_BLOCK)
        dst = live(m2g_own_dst[:, pl.ds(start, EDGE_BLOCK)], back_length, start)
        src = m2g_own_src[:, pl.ds(start, EDGE_BLOCK)]
        back_acc[...] += dot_nt(one_hot_t(dst, grid_rows), one_hot_t(src, mesh_rows))
        return carry

    lax.fori_loop(0, m2g_own_src.shape[1] // EDGE_BLOCK, own_back, 0)
    back[...] = back_acc[...].astype(BF)

    wwait(2, "cd")
    wstart(2, "g")

    wwait(1, "efg")
    hidden = down_w.shape[1]
    for j in range(down_w.shape[0]):
        up = up_w[:, :, j * hidden : (j + 1) * hidden].reshape(width, hidden)
        expanded[j] = silu(dot(normed_two, up)).astype(BF)
    total = after_attn + dot(expanded[me], down_w[me])
    for kind, slot in (("e", xm), ("f", ym), ("g", dm)):
        wwait(2, kind)
        total = total + dot(expanded[slot], down_w[slot])
    mesh_out = total.astype(BF)
    return_rows = dot(mesh_out, w_return[...]).astype(BF)
    ret_up[...] = dot(one_hot(m2g_src[0, pl.ds(upper, 1), :], mesh_rows), return_rows).astype(BF)
    ret_dn[...] = dot(one_hot(m2g_src[0, pl.ds(lower, 1), :], mesh_rows), return_rows).astype(BF)

    @pl.when(has_upper)
    def _():
        message(2, ret_up, back_lo, upper).start()

    @pl.when(has_lower)
    def _():
        message(3, ret_dn, back_hi, lower).start()

    def skip_rows(i, carry):
        rows = pl.ds(pl.multiple_of(i * block, block), block)
        skip[rows, :] = dot(latent[rows, :], w_skip[...])
        return carry

    lax.fori_loop(0, grid_rows // block, skip_rows, 0)
    agg = dot(back[...], return_rows)
    blen_lo = jnp.where(has_lower, m2g_len[0, lower], 0)
    blen_hi = jnp.where(has_upper, m2g_len[0, upper], 0)
    land_lo = one_hot_t(live(m2g_dst[0, pl.ds(lower, 1), :], blen_lo), grid_rows)
    land_hi = one_hot_t(live(m2g_dst[0, pl.ds(upper, 1), :], blen_hi), grid_rows)

    @pl.when(has_lower)
    def _():
        message(2, ret_up, back_lo, upper).wait_recv()

    @pl.when(has_upper)
    def _():
        message(3, ret_dn, back_hi, lower).wait_recv()

    @pl.when(jnp.logical_not(has_lower))
    def _():
        back_lo[...] = jnp.zeros_like(back_lo)

    @pl.when(jnp.logical_not(has_upper))
    def _():
        back_hi[...] = jnp.zeros_like(back_hi)

    agg = agg + dot(land_lo, back_lo[...]) + dot(land_hi, back_hi[...])
    pre = dot(agg.astype(BF), w_grid[...]) + skip[...]
    updated = silu(pre).astype(BF)
    out[...] = dot_nt(head[...], updated).astype(BF)

    for group in range(3):
        for kind in "abcdefg":
            wcopy(group, kind).wait_send()
    for off in range(1, bands):
        halo(off).wait_send()

    @pl.when(has_upper)
    def _():
        message(0, pick_up, from_lo, upper).wait_send()
        message(2, ret_up, back_lo, upper).wait_send()

    @pl.when(has_lower)
    def _():
        message(1, pick_dn, from_hi, lower).wait_send()
        message(3, ret_dn, back_hi, lower).wait_send()


NAMES = (
    "grid_in", "mesh_embed", "g2m_src", "g2m_dst", "g2m_own_src", "g2m_own_dst", "g2m_len",
    "mesh_nbr", "halo_rows", "m2g_src", "m2g_dst", "m2g_own_src", "m2g_own_dst", "m2g_len",
    "w_embed", "w_send", "w_mesh", "attn_gain", "w_query", "w_key", "w_value", "w_project",
    "mlp_gain", "w_up", "w_down", "w_return", "w_grid", "w_skip", "w_out",
)
SHARDED = ("w_query", "w_key", "w_value", "w_project", "w_up", "w_down")
STAGED = tuple(n for n in NAMES[:-1] if n not in SHARDED)
SCALARS = ("g2m_len", "halo_rows", "m2g_len")
FIRST = ("w_query", "w_key", "w_value", "w_project", "grid_in", "w_embed", "w_send", "g2m_src")
FETCH_ORDER = FIRST + ("w_up", "w_down") + tuple(
    n for n in STAGED if n not in FIRST
)


def shards(*args):
    args = list(args)
    for name in ("g2m_len", "m2g_len", "mesh_nbr", "w_out"):
        i = NAMES.index(name)
        args[i] = args[i].T
    for name in ("attn_gain", "mlp_gain"):
        i = NAMES.index(name)
        args[i] = args[i].reshape(1, -1)
    grid_rows = args[0].shape[1]
    mesh_rows, width = args[1].shape
    slots = args[2].shape[2]
    hb = args[8].shape[1]
    bands = lax.axis_size("space")
    members = lax.axis_size("member")
    depth, ffn = args[23].shape
    down = args[24].shape
    f_out = args[28].shape[0]
    named = dict(zip(NAMES, args))
    staging = [
        (pltpu.SMEM if n in SCALARS else pltpu.VMEM)(named[n].shape, named[n].dtype)
        for n in STAGED
    ]
    msg = pltpu.VMEM((slots, width), BF)
    in_specs = [pl.BlockSpec(memory_space=pltpu.HBM)] * (len(args) - 1)
    in_specs.append(pl.BlockSpec(memory_space=pltpu.VMEM))
    result = pl.pallas_call(
        functools.partial(kernel, bands),
        out_shape=jax.ShapeDtypeStruct((f_out, grid_rows), BF),
        in_specs=in_specs,
        out_specs=pl.BlockSpec(memory_space=pltpu.VMEM),
        scratch_shapes=staging + [
            pltpu.VMEM((members, 4, depth, width), BF),
            pltpu.VMEM((members, depth, ffn), BF),
            pltpu.VMEM((members,) + tuple(down), BF),
            pltpu.VMEM((grid_rows, width), BF),
            pltpu.VMEM((grid_rows, width), BF),
            pltpu.VMEM((mesh_rows, grid_rows), BF),
            pltpu.VMEM((mesh_rows, grid_rows), F32),
            pltpu.VMEM((grid_rows, mesh_rows), BF),
            pltpu.VMEM((grid_rows, mesh_rows), F32),
            pltpu.VMEM((grid_rows, width), F32),
            msg, msg, msg, msg, msg, msg, msg, msg,
            pltpu.VMEM((bands * hb, width), BF),
            pltpu.VMEM((members, mesh_rows, down[0]), BF),
            pltpu.SemaphoreType.DMA((3, 7)),
            pltpu.SemaphoreType.DMA((3, 7)),
            pltpu.SemaphoreType.DMA((4,)),
            pltpu.SemaphoreType.DMA((4,)),
            pltpu.SemaphoreType.DMA((bands,)),
            pltpu.SemaphoreType.DMA((bands,)),
            pltpu.SemaphoreType.DMA((len(NAMES),)),
        ],
        compiler_params=pltpu.CompilerParams(
            collective_id=0, has_side_effects=True, vmem_limit_bytes=66060288
        ),
        cost_estimate=pl.CostEstimate(
            flops=8_000_000_000, bytes_accessed=6_000_000, transcendentals=3_000_000
        ),
    )(*args)
    return result[None]


def solution(mesh):
    placed = (
        P("member", "space", None),
        P("space", None),
        P("space", None, None),
        P("space", None, None),
        P("space", None),
        P("space", None),
        P(None, "space"),
        P("space", None),
        P("space", None),
        P("space", None, None),
        P("space", None, None),
        P("space", None),
        P("space", None),
        P(None, "space"),
        P(),
        P(),
        P(),
        P(),
        P("member", None),
        P("member", None),
        P("member", None),
        P("member", None),
        P(),
        P("member", None),
        P("member", None),
        P(),
        P(),
        P(),
        P(),
    )
    return jax.shard_map(
        shards, mesh=mesh, in_specs=placed, out_specs=P("member", None, "space"), check_vma=False
    )
```
